256 devices in a mesh: row: 32 (over z, x_hi, core), key: 8 (over y, x_lo).
Axes of the slice: x: 4 (x_hi: 2, x_lo: 2; x = x_hi * 2 + x_lo), y: 4, z: 8, core: 2. Of those that a mesh axis runs over, the one named last changes fastest.
Arguments:
- query: bfloat16 [160, 2048, 128], P('row', 'key'), may hold values from -6 to 6
- key_in: bfloat16 [160, 2048, 128], P('row', 'key'), may hold values from -6 to 6
- value: bfloat16 [160, 2048, 128], P('row', 'key'), may hold values from -6 to 6
- output: bfloat16 [160, 2048, 128], P('row', 'key'), may hold values from -3 to 3
- dout: bfloat16 [160, 2048, 128], P('row', 'key'), may hold values from -192 to 192
- lse: float32 [4, 160, 2048], P(None, 'row', 'key'), may hold values from 8 to 9
- bias: float32 [4, 2048, 2048], P(None, 'key', 'row'), may hold values from -6 to 6
- mask: int32 [2048], replicated, may hold values 0 or 1
Outputs:
- grad_query: float32 [160, 2048, 128], P('row', 'key')
- grad_key: float32 [160, 2048, 128], P('row', 'key')
- grad_value: float32 [160, 2048, 128], P('row', 'key')
- grad_bias: float32 [4, 2048, 2048], P(None, 'key', 'row')
The draws below stay inside these ranges and needn't reach their ends.
All inputs are finite; a program needn't handle non-finite values.
Results may differ from the reference program's by a relative error of at most 0.011.
Values may be sent and summed in bfloat16 or wider, within the bound.
A program may use at most 128 MiB of HBM per device.

```python
import jax
import jax.numpy as jnp
from jax import lax

H = 4
DH = 32
C = 128
N = 2048
SLAB = 160


def touch_ends(drawn, own_key, least, largest):
    dims = drawn.shape
    place = [jax.random.randint(jax.random.fold_in(own_key, axis), (), 0, dims[axis]) for axis in range(len(dims))]
    drawn = drawn.at[tuple(place)].set(least)
    longest = dims.index(max(dims))
    place[longest] = (place[longest] + 1) % dims[longest]
    return drawn.at[tuple(place)].set(largest)


def steps_of(own_key, dims, pieces, low, largest):
    def one(position, shards_of):
        steps = jax.random.uniform(jax.random.fold_in(jax.random.fold_in(own_key, 6), position), (shards_of,), jnp.float32, low / len(pieces), largest / len(pieces))
        return jnp.repeat(jnp.exp(steps), dims[position] // shards_of).reshape((-1,) + (1,) * (len(dims) - position - 1))

    level = one(*pieces[0])
    for cut in pieces[1:]:
        level = level * one(*cut)
    return level


def bell_draw(stream_key, dims, spread, bound, split=(), kind=jnp.bfloat16):
    factor_of = steps_of(stream_key, dims, split, -0.22, 0.18) if split else 1.0
    array = jax.random.normal(stream_key, dims, jnp.float32) * spread * factor_of
    return jnp.minimum(jnp.maximum(array, -bound), bound).astype(kind)


def setup_inputs(seed: int = 0) -> dict:
    splits = jax.random.split(jax.random.key(seed), 9)
    query = bell_draw(splits[0], (SLAB, N, C), 1.0, 6.0, ((0, 32), (1, 8)))
    key_in = bell_draw(splits[1], (SLAB, N, C), 1.0, 6.0, ((0, 32), (1, 8)))
    value = bell_draw(splits[2], (SLAB, N, C), 1.0, 6.0, ((0, 32), (1, 8)))
    output = bell_draw(splits[3], (SLAB, N, C), 0.5, 3.0, ((0, 32), (1, 8)))
    dout = bell_draw(splits[4], (SLAB, N, C), 32.0, 192.0, ((0, 32), (1, 8)))
    lse = jnp.clip(8.0 + 1.0 * jax.random.uniform(splits[5], (H, SLAB, N), jnp.float32) ** steps_of(splits[5], (H, SLAB, N), ((1, 32), (2, 8)), -0.2, 0.2), 8.0, 9.0)
    bias = bell_draw(splits[6], (H, N, N), 1.0, 6.0, ((1, 8), (2, 32)), jnp.float32)
    mask = touch_ends((jax.random.randint(splits[7], (N,), 0, 8) < 7).astype(jnp.int32), jax.random.fold_in(splits[7], 1), 0, 1)
    return {"query": query, "key_in": key_in, "value": value, "output": output, "dout": dout, "lse": lse, "bias": bias, "mask": mask}


def row_grads(query_row, key_row, value_row, output_row, dout_row, lse_row, bias_full, key_keep):
    score_scale = DH ** -0.5
    q_heads = query_row.astype(jnp.float32).reshape(N, H, DH)
    k_heads = key_row.astype(jnp.float32).reshape(N, H, DH)
    v_heads = value_row.astype(jnp.float32).reshape(N, H, DH)
    o_heads = output_row.astype(jnp.float32).reshape(N, H, DH)
    d_heads = dout_row.astype(jnp.float32).reshape(N, H, DH)
    logits = jnp.einsum("qhd,khd->hqk", q_heads, k_heads) * score_scale + bias_full
    row_probs = jnp.where(key_keep[None, None, :], jnp.exp(logits - lse_row[:, :, None]), 0.0)
    probs_low = lax.optimization_barrier(row_probs.astype(jnp.bfloat16)).astype(jnp.float32)
    delta = jnp.transpose(jnp.sum(d_heads * o_heads, axis=2))
    dprobs = jnp.einsum("qhd,khd->hqk", d_heads, v_heads)
    dlogits = row_probs * (dprobs - delta[:, :, None])
    dlogits_low = lax.optimization_barrier(dlogits.astype(jnp.bfloat16)).astype(jnp.float32)
    grad_q = score_scale * jnp.einsum("hqk,khd->qhd", dlogits_low, k_heads)
    grad_k = score_scale * jnp.einsum("hqk,qhd->khd", dlogits_low, q_heads)
    grad_v = jnp.einsum("hqk,qhd->khd", probs_low, d_heads)
    return grad_q.reshape(N, C), grad_k.reshape(N, C), grad_v.reshape(N, C), dlogits


def reference(query, key_in, value, output, dout, lse, bias, mask):
    key_keep = mask == 1
    lse_rows = jnp.transpose(lse, (1, 0, 2))

    def one_row(summed, row_items):
        query_row, key_row, value_row, output_row, dout_row, lse_row = row_items
        grad_q, grad_k, grad_v, dlogits = row_grads(query_row, key_row, value_row, output_row, dout_row, lse_row, bias, key_keep)
        return summed + dlogits, (grad_q, grad_k, grad_v)

    summed, (grad_query, grad_key, grad_value) = lax.scan(
        one_row, jnp.zeros((H, N, N), jnp.float32), (query, key_in, value, output, dout, lse_rows))
    return grad_query, grad_key, grad_value, summed
```

```python
import jax
import jax.numpy as jnp
from jax import lax
from jax.experimental import pallas as pl
from jax.experimental.pallas import tpu as pltpu
from jax.sharding import PartitionSpec as P

MESH = pl.DeviceIdType.MESH
f32, bf16 = jnp.float32, jnp.bfloat16

H, DH, NR = 4, 32, 5
QB = 256
NY, NZ = 4, 8
NJ = NY * QB
KB = 128
JT = 512
SHIFT = 6.0
LOG2E = 1.4426950408889634
SCALE = DH**-0.5
NEG = -1e30


def pieces(a):
    first = a.astype(bf16).astype(f32)
    rest = a - first
    second = rest.astype(bf16).astype(f32)
    return first, second, rest - second


def aligned(start, size):
    return pl.ds(pl.multiple_of(start, size), size)


def kernel(
    q_ref, k_ref, v_ref, o_ref, do_ref, lse_ref, bias_ref, mask_ref,
    gq_ref, gk_ref, gv_ref, gb_ref,
    se, sx, sy, er, xr, yr, lt, gb, own, sr, sl, rr, rl, gqa, sg, gkvr, gqc, sgq, gqr, xs, xg, sb, gbr,
    e_s, e_r, x_s, x_r, c_s, c_r, y_s, y_r, h_s, h_r, fr_s, fr_r, fl_s, fl_r,
    rr_s, rr_r, rl_s, rl_r, g_s, g_r, qc_s, qc_r, qy_s, qy_r, xg_s, xg_r, b_s, b_r, loc,
):
    r, b = lax.axis_index("row"), lax.axis_index("key")
    z, xh, c = r // 4, (r // 2) % 2, r % 2
    y, xl = b // 2, b % 2

    def row_of(zz, xx, cc):
        return zz * 4 + xx * 2 + cc

    def remote(src, dst, s_sem, r_sem, row, key):
        return pltpu.make_async_remote_copy(
            src_ref=src, dst_ref=dst, send_sem=s_sem, recv_sem=r_sem,
            device_id=(row, key), device_id_type=MESH,
        )

    right = row_of((z + 1) % NZ, xh, c)
    left = row_of((z + NZ - 1) % NZ, xh, c)
    across = row_of(z, 1 - xh, c)
    other = row_of(z, xh, 1 - c)
    sends = []

    barrier = pltpu.get_barrier_semaphore()
    for row in (right, left, across):
        pl.semaphore_signal(barrier, inc=1, device_id=(row, b), device_id_type=MESH)
    for n in range(1, 16):
        dy, dc, dx = n // 4, (n // 2) % 2, n % 2
        pl.semaphore_signal(
            barrier, inc=1,
            device_id=(row_of(z, xh, c ^ dc), ((y + dy) % NY) * 2 + (xl ^ dx)),
            device_id_type=MESH,
        )

    for h in range(H):
        se[h] = jnp.exp(bias_ref[h] + SHIFT).T.astype(bf16)

    pl.semaphore_wait(barrier, 18)

    mine = pl.ds(pl.multiple_of(xh * 64, 64), 64)
    lanes = aligned(y * QB, QB)
    rows = pl.ds(c * NR, NR)

    e_copies = []
    for d in range(1, NY):
        yy = (y + d) % NY
        cp = remote(se.at[yy], er.at[z, mine, lanes], e_s.at[d], e_r.at[d], r, yy * 2 + xl)
        cp.start()
        e_copies.append(cp)
    e_own = pltpu.make_async_copy(se.at[y], er.at[z, mine, lanes], loc.at[0])
    e_own.start()

    place = lax.broadcasted_iota(jnp.int32, (16, QB), 0)

    def prep_x(i, carry):
        qt = q_ref[i].astype(f32).T
        dot_ = do_ref[i].astype(f32)
        dt = dot_.T
        prod = (dot_ * o_ref[i].astype(f32)).T
        for h in range(H):
            hs = slice(h * DH, (h + 1) * DH)
            l1, l2, l3 = pieces((lse_ref[h, pl.ds(i, 1), :] + SHIFT) * LOG2E)
            d1, d2, d3 = pieces(jnp.sum(prod[hs], axis=0, keepdims=True))
            aux = jnp.where(place == 6, 1.0, 0.0)
            for n, piece in enumerate((l1, l2, l3, d1, d2, d3)):
                aux = jnp.where(place == n, piece, aux)
            sx[h, i, 0:32] = qt[hs].astype(bf16)
            sx[h, i, 32:64] = dt[hs].astype(bf16)
            sx[h, i, 64:80] = aux.astype(bf16)
        return carry

    lax.fori_loop(0, NR, prep_x, 0)

    x_copies = []
    for d in range(1, NY):
        yy = (y + d) % NY
        cp = remote(sx.at[yy], xr.at[rows, 32:112, lanes], x_s.at[d], x_r.at[d], r, yy * 2 + xl)
        cp.start()
        x_copies.append(cp)
    x_own = pltpu.make_async_copy(sx.at[y], xr.at[rows, 32:112, lanes], loc.at[1])
    x_own.start()

    for cp in e_copies:
        cp.wait_recv()
    e_own.wait()
    h_copy = remote(er.at[z, mine], er.at[z, mine], h_s, h_r, across, b)
    h_copy.start()

    def prep_y(i, carry):
        for ref, lo in ((k_ref, 0), (v_ref, 32)):
            full = ref[i].astype(f32)
            for cc in range(2):
                part = jnp.concatenate(
                    [full[cc * 64 : cc * 64 + 64], full[128 + cc * 64 : 192 + cc * 64]], 0
                ).T
                for h in range(H):
                    sy[h, cc, i, lo : lo + 32] = part[h * DH : (h + 1) * DH].astype(bf16)
        return carry

    lax.fori_loop(0, NR, prep_y, 0)

    y_copies = []
    for n in range(1, 16):
        dy, dc, dx = n // 4, (n // 2) % 2, n % 2
        yy, cc = (y + dy) % NY, c ^ dc
        cp = remote(
            sy.at[yy, cc], yr.at[b, rows], y_s.at[n], y_r.at[n],
            row_of(z, xh, cc), yy * 2 + (xl ^ dx),
        )
        cp.start()
        y_copies.append(cp)
    y_own = pltpu.make_async_copy(sy.at[y, c], yr.at[b, rows], loc.at[2])
    y_own.start()

    h_copy.wait_recv()

    def ring(step):
        going_r, going_l = (z + NZ - step) % NZ, (z + step) % NZ
        if step < 3:
            src_r, src_l = er.at[going_r], er.at[going_l]
        else:
            src_r, src_l = er.at[going_r, 0:64], er.at[going_l, 64:128]
        cr = remote(src_r, src_r, fr_s.at[step], fr_r.at[step], right, b)
        cl = remote(src_l, src_l, fl_s.at[step], fl_r.at[step], left, b)
        cr.start()
        cl.start()
        return cr, cl

    ring_copies = [ring(0)]

    c_copies = []
    x_own.wait()
    for d in range(NY):
        if d:
            x_copies[d - 1].wait_recv()
        part = xr.at[rows, 32:112, aligned(((y + NY - d) % NY) * QB, QB)]
        cp = remote(part, part, c_s.at[d], c_r.at[d], other, b)
        cp.start()
        c_copies.append(cp)

    for step in range(1, 4):
        for cp in ring_copies[-1]:
            cp.wait_recv()
        ring_copies.append(ring(step))

    gqa[...] = jnp.zeros_like(gqa)
    for cp in c_copies:
        cp.wait_recv()

    def twice(i, carry):
        xr[i, 0:32, :] = xr[i, 32:64, :]
        xr[i, 112:128, :] = jnp.zeros((16, NJ), bf16)
        return carry

    lax.fori_loop(0, 2 * NR, twice, 0)
    for cp in y_copies:
        cp.wait_recv()
    y_own.wait()
    for cp in ring_copies[-1]:
        cp.wait_recv()

    spot = lax.broadcasted_iota(jnp.int32, (32, 2 * KB), 0)

    def score_rows(m, z_a, z_b):
        gb[...] = jnp.zeros_like(gb)
        neg = jnp.concatenate([mask_ref[c, z_a], mask_ref[c, z_b]], 1)
        aux_t = jnp.where(spot < 3, -1.0, jnp.where(spot == 6, neg, 0.0)).astype(bf16)
        aux_d = jnp.where((spot >= 3) & (spot < 6), -1.0, 0.0).astype(bf16)
        zero = jnp.zeros((32, 2 * KB), bf16)

        def one_row(i, carry):
            both = jnp.concatenate([yr[z_a, i], yr[z_b, i]], 1)
            kt, vt = both[0:32], both[32:64]
            scaled = kt.astype(f32) * (SCALE * LOG2E)
            high = scaled.astype(bf16)
            low = (scaled - high.astype(f32)).astype(bf16)
            lhs_t = jnp.concatenate([high, low, zero, aux_t], 0)
            lhs_d = jnp.concatenate([zero, zero, vt, aux_d], 0)
            lt[...] = jnp.concatenate([lhs_t, lhs_d], 1).T
            gk = gv = None
            for jt in range(NJ // JT):
                js = slice(jt * JT, (jt + 1) * JT)
                x = xr[i, :, js]
                td = jnp.dot(lt[...], x, preferred_element_type=f32)
                e = jnp.concatenate([er[z_a, :, js], er[z_b, :, js]], 0).astype(f32)
                p = jnp.exp2(td[: 2 * KB]) * e
                ds = p * td[2 * KB :]
                gb[:, js] += ds
                pb, db = p.astype(bf16), ds.astype(bf16)
                last = (((1,), (1,)), ((), ()))
                gvj = lax.dot_general(x[64:96], pb, last, preferred_element_type=f32)
                gkj = lax.dot_general(x[0:32], db, last, preferred_element_type=f32)
                gk, gv = (gkj, gvj) if jt == 0 else (gk + gkj, gv + gvj)
                gqa[i, :, js] += jnp.dot(kt, db, preferred_element_type=f32)
            out = jnp.concatenate([gk * SCALE, gv], 0).astype(bf16)
            sg[m, 0, i] = out[:, :KB]
            sg[m, 1, i] = out[:, KB:]
            return carry

        lax.fori_loop(0, 2 * NR, one_row, 0, unroll=2)

    me = y * 4 + c * 2 + xl

    def return_keys(m, half, zz):
        for cc in range(2):
            is_self = (zz == b) & (c == cc)
            src, dst = sg.at[m, half, cc * NR : (cc + 1) * NR], gkvr.at[me]

            @pl.when(jnp.logical_not(is_self))
            def _():
                remote(src, dst, g_s.at[m, half, cc], g_r.at[me], row_of(z, xh, cc), zz).start()

            @pl.when(is_self)
            def _():
                cp = pltpu.make_async_copy(src, dst, loc.at[3])
                cp.start()
                cp.wait()

    def drain_keys(m, half, zz):
        for cc in range(2):
            is_self = (zz == b) & (c == cc)
            src, dst = sg.at[m, half, cc * NR : (cc + 1) * NR], gkvr.at[me]

            @pl.when(jnp.logical_not(is_self))
            def _():
                remote(src, dst, g_s.at[m, half, cc], g_r.at[me], row_of(z, xh, cc), zz).wait_send()

    blocks = [((z + 4 - m) % NZ, (z + 4 + m) % NZ if m else z) for m in range(4)]
    rs_copies = []
    for m in range(4):
        z_a, z_b = blocks[m]
        score_rows(m, z_a, z_b)
        if m == 0:
            own[...] = gb[KB:, :]
            sr[0, 0:64] = gb[0:64, :].astype(bf16)
            sl[0, 64:128] = gb[64:128, :].astype(bf16)
            cr = remote(sr.at[0, 0:64], rr.at[0, 0:64], rr_s.at[0], rr_r.at[0], right, b)
            cl = remote(sl.at[0, 64:128], rl.at[0, 64:128], rl_s.at[0], rl_r.at[0], left, b)
        else:
            for cp in rs_copies[-1]:
                cp.wait_recv()
            if m == 1:
                sr[m, 0:64] = (gb[0:64, :] + rr[0, 0:64].astype(f32)).astype(bf16)
                sr[m, 64:128] = gb[64:128, :].astype(bf16)
                sl[m, 0:64] = gb[128:192, :].astype(bf16)
                sl[m, 64:128] = (gb[192:256, :] + rl[0, 64:128].astype(f32)).astype(bf16)
            else:
                sr[m] = (gb[0:KB, :] + rr[m - 1].astype(f32)).astype(bf16)
                sl[m] = (gb[KB:, :] + rl[m - 1].astype(f32)).astype(bf16)
            cr = remote(sr.at[m], rr.at[m], rr_s.at[m], rr_r.at[m], right, b)
            cl = remote(sl.at[m], rl.at[m], rl_s.at[m], rl_r.at[m], left, b)
        cr.start()
        cl.start()
        rs_copies.append((cr, cl))
        return_keys(m, 0, z_a)
        return_keys(m, 1, z_b)

    theirs = pl.ds((1 - c) * NR, NR)
    qc_copy = remote(gqa.at[theirs], gqc, qc_s, qc_r, other, b)
    qc_copy.start()
    qc_copy.wait_recv()

    def add_q(i, carry):
        total = ((gqa[c * NR + i] + gqc[i]) * SCALE).astype(bf16)
        for n in range(NY):
            sgq[n, i] = total[:, n * QB : (n + 1) * QB]
        return carry

    lax.fori_loop(0, NR, add_q, 0)
    q_copies = []
    for d in range(1, NY):
        yy = (y + d) % NY
        cp = remote(sgq.at[yy], gqr.at[y], qy_s.at[d], qy_r.at[d], r, yy * 2 + xl)
        cp.start()
        q_copies.append(cp)
    gqr[y] = sgq[y]

    for cp in rs_copies[-1]:
        cp.wait_recv()
    across_rows = pl.ds(pl.multiple_of((1 - xh) * 64, 64), 64)
    xs[...] = (
        own[across_rows, :] + rr[3, across_rows, :].astype(f32) + rl[3, across_rows, :].astype(f32)
    ).astype(bf16)
    xg_copy = remote(xs, xg, xg_s, xg_r, across, b)
    xg_copy.start()
    own[mine, :] = own[mine, :] + rr[3, mine, :].astype(f32) + rl[3, mine, :].astype(f32)

    for n in range(16):

        @pl.when(n != me)
        def _(n=n):
            remote(sg.at[0, 0, 0:NR], gkvr.at[n], g_s.at[0, 0, 0], g_r.at[n], r, b).wait_recv()

    def keys_home(i, carry):
        for cc in range(2):
            for ref, lo in ((gk_ref, 0), (gv_ref, 32)):
                heads = [
                    gkvr[h * 4 + cc * 2, i, lo : lo + 32].astype(f32)
                    + gkvr[h * 4 + cc * 2 + 1, i, lo : lo + 32].astype(f32)
                    for h in range(H)
                ]
                part = jnp.concatenate(heads, 0).T
                ref[i, cc * 64 : cc * 64 + 64] = part[0:64]
                ref[i, 128 + cc * 64 : 192 + cc * 64] = part[64:128]
        return carry

    lax.fori_loop(0, NR, keys_home, 0)

    xg_copy.wait_recv()
    total = (own[mine, :] + xg[...].astype(f32)).astype(bf16)
    for n in range(NY):
        sb[n] = total[:, n * QB : (n + 1) * QB]
    b_copies = []
    for d in range(1, NY):
        yy = (y + d) % NY
        cp = remote(sb.at[yy], gbr.at[y], b_s.at[d], b_r.at[d], r, yy * 2 + xl)
        cp.start()
        b_copies.append(cp)
    gbr[y] = sb[y]

    for cp in q_copies:
        cp.wait_recv()

    def query_home(i, carry):
        gq_ref[i] = jnp.concatenate([gqr[h, i].astype(f32) for h in range(H)], 0).T
        return carry

    lax.fori_loop(0, NR, query_home, 0)

    for cp in b_copies:
        cp.wait_recv()
    for h in range(H):
        gb_ref[h] = gbr[h].astype(f32).T

    for m in range(4):
        drain_keys(m, 0, blocks[m][0])
        drain_keys(m, 1, blocks[m][1])
    for cp in [h_copy, qc_copy, xg_copy, *e_copies, *x_copies, *y_copies, *c_copies, *q_copies, *b_copies]:
        cp.wait_send()
    for pair in (*ring_copies, *rs_copies):
        for cp in pair:
            cp.wait_send()


def per_device(query, key_in, value, output, dout, lse, bias, mask):
    neg = jnp.where(mask == 1, 0.0, NEG).astype(f32)
    neg = neg.reshape(NZ, 2, 2, 64).transpose(2, 0, 1, 3).reshape(2, NZ, 1, KB)
    dma = pltpu.SemaphoreType.DMA
    grad = jax.ShapeDtypeStruct(query.shape, f32)
    vmem = pl.BlockSpec(memory_space=pltpu.VMEM)
    scratch = [
        pltpu.VMEM((H, 64, QB), bf16),
        pltpu.VMEM((H, NR, 80, QB), bf16),
        pltpu.VMEM((H, 2, NR, 64, KB), bf16),
        pltpu.VMEM((NZ, KB, NJ), bf16),
        pltpu.VMEM((2 * NR, 128, NJ), bf16),
        pltpu.VMEM((NZ, 2 * NR, 64, KB), bf16),
        pltpu.VMEM((4 * KB, 128), bf16),
        pltpu.VMEM((2 * KB, NJ), f32),
        pltpu.VMEM((KB, NJ), f32),
        pltpu.VMEM((4, KB, NJ), bf16),
        pltpu.VMEM((4, KB, NJ), bf16),
        pltpu.VMEM((4, KB, NJ), bf16),
        pltpu.VMEM((4, KB, NJ), bf16),
        pltpu.VMEM((2 * NR, DH, NJ), f32),
        pltpu.VMEM((4, 2, 2 * NR, 64, KB), bf16),
        pltpu.VMEM((16, NR, 64, KB), bf16),
        pltpu.VMEM((NR, DH, NJ), f32),
        pltpu.VMEM((NY, NR, DH, QB), bf16),
        pltpu.VMEM((NY, NR, DH, QB), bf16),
        pltpu.VMEM((64, NJ), bf16),
        pltpu.VMEM((64, NJ), bf16),
        pltpu.VMEM((NY, 64, QB), bf16),
        pltpu.VMEM((NY, 64, QB), bf16),
    ]
    sems = [
        dma((4,)), dma((4,)), dma((4,)), dma((4,)), dma((4,)), dma((4,)), dma((16,)), dma((16,)),
        dma, dma, dma((4,)), dma((4,)), dma((4,)), dma((4,)),
        dma((4,)), dma((4,)), dma((4,)), dma((4,)), dma((4, 2, 2)), dma((16,)), dma, dma,
        dma((4,)), dma((4,)), dma, dma, dma((4,)), dma((4,)), dma((4,)),
    ]
    return pl.pallas_call(
        kernel,
        out_shape=[grad, grad, grad, jax.ShapeDtypeStruct(bias.shape, f32)],
        in_specs=[vmem] * 8,
        out_specs=[vmem] * 4,
        scratch_shapes=scratch + sems,
        compiler_params=pltpu.CompilerParams(
            collective_id=0, has_side_effects=True, vmem_limit_bytes=56 << 20
        ),
    )(query, key_in, value, output, dout, lse, bias, neg)


def solution(mesh):
    in_specs = (
        P("row", "key", None),
        P("row", "key", None),
        P("row", "key", None),
        P("row", "key", None),
        P("row", "key", None),
        P(None, "row", "key"),
        P(None, "key", "row"),
        P(),
    )
    out_specs = (
        P("row", "key", None),
        P("row", "key", None),
        P("row", "key", None),
        P(None, "key", "row"),
    )
    return jax.shard_map(
        per_device, mesh=mesh, in_specs=in_specs, out_specs=out_specs, check_vma=False
    )
```

```python
import jax
import jax.numpy as jnp
from jax import lax
from jax.experimental import pallas as pl
from jax.experimental.pallas import tpu as pltpu
from jax.sharding import PartitionSpec as P

MESH = pl.DeviceIdType.MESH
f32, bf16 = jnp.float32, jnp.bfloat16

H, DH, NR = 4, 32, 5
QB = 256
NY, NZ = 4, 8
NJ = NY * QB
HJ = NJ // 2
KB = 128
SHIFT = 6.0
LOG2E = 1.4426950408889634
SCALE = DH**-0.5
NEG = -1e30


def pieces(a):
    first = a.astype(bf16).astype(f32)
    rest = a - first
    second = rest.astype(bf16).astype(f32)
    return first, second, rest - second


def aligned(start, size):
    return pl.ds(pl.multiple_of(start, size), size)


def kernel(
    q_ref, k_ref, v_ref, o_ref, do_ref, lse_ref, bias_ref, mask_ref,
    gqr, gkvr, gbr,
    se, sx, sy, er, xr, yr, neg, lt, gb, own, sr, sl, rr, rl, gqa, gka, sg, pr, gqc, sgq, sb,
    e_s, e_r, x_s, x_r, c_s, c_r, y_s, y_r, w_s, w_r, fr_s, fr_r, fl_s, fl_r,
    rr_s, rr_r, rl_s, rl_r, p_s, p_r, g_s, g_r, qc_s, qc_r, qy_s, qy_r, b_s, b_r, loc,
):
    r, b = lax.axis_index("row"), lax.axis_index("key")
    z, xh, c = r // 4, (r // 2) % 2, r % 2
    y, xl = b // 2, b % 2

    def row_of(zz, xx, cc):
        return zz * 4 + xx * 2 + cc

    def remote(src, dst, s_sem, r_sem, row, key):
        return pltpu.make_async_remote_copy(
            src_ref=src, dst_ref=dst, send_sem=s_sem, recv_sem=r_sem,
            device_id=(row, key), device_id_type=MESH,
        )

    right = row_of((z + 1) % NZ, xh, c)
    left = row_of((z + NZ - 1) % NZ, xh, c)
    across = row_of(z, 1 - xh, c)
    other = row_of(z, xh, 1 - c)
    done = []

    barrier = pltpu.get_barrier_semaphore()
    greet = [(right, b), (left, b)]
    greet += [(across, ((y + d) % NY) * 2 + xl) for d in range(NY)]
    greet += [
        (row_of(z, xh, c ^ ((n // 2) % 2)), ((y + n // 4) % NY) * 2 + (xl ^ (n % 2)))
        for n in range(1, 16)
    ]
    for device in greet:
        pl.semaphore_signal(barrier, inc=1, device_id=device, device_id_type=MESH)

    for h in range(H):
        se[h] = jnp.exp(bias_ref[h] + SHIFT).astype(bf16)

    pl.semaphore_wait(barrier, len(greet))

    mine = aligned(xh * 64, 64)
    lanes = aligned(y * QB, QB)
    lanes_e = aligned((y % 2) * QB, QB)
    rows = pl.ds(c * NR, NR)

    e_place = er.at[y // 2, z, mine, lanes_e]
    e_copies = []
    for n in (1, 3, 2, 4, 5, 7, 6):
        yy = (y + n % 4) % NY
        cp = remote(
            se.at[yy], e_place, e_s.at[n], e_r.at[n], row_of(z, xh ^ (n // 4), c), yy * 2 + xl
        )
        cp.start()
        e_copies.append(cp)
    e_own = pltpu.make_async_copy(se.at[y], e_place, loc.at[0])
    e_own.start()

    def prep_y(i, carry):
        for ref, lo in ((k_ref, 0), (v_ref, 32)):
            full = ref[i].astype(f32)
            for cc in range(2):
                part = jnp.concatenate(
                    [full[cc * 64 : cc * 64 + 64], full[128 + cc * 64 : 192 + cc * 64]], 0
                ).T
                for h in range(H):
                    sy[h, cc, i, lo : lo + 32] = part[h * DH : (h + 1) * DH].astype(bf16)
        return carry

    lax.fori_loop(0, NR, prep_y, 0)

    y_copies = {}
    for n in (1, 2, 3, 6, 7, 4, 5):
        d, dc = n // 2, n % 2
        yy, cc = (y + d) % NY, c ^ dc
        cp = remote(
            sy.at[yy, cc], yr.at[b, rows], y_s.at[n], y_r.at[n], row_of(z, xh, cc), yy * 2 + xl
        )
        cp.start()
        y_copies[n] = cp
    y_own = pltpu.make_async_copy(sy.at[y, c], yr.at[b, rows], loc.at[2])
    y_own.start()

    place = lax.broadcasted_iota(jnp.int32, (16, QB), 0)

    def prep_x(i, carry):
        qt = q_ref[i].astype(f32).T
        d_out = do_ref[i].astype(f32)
        dt = d_out.T
        prod = (d_out * o_ref[i].astype(f32)).T
        for h in range(H):
            hs = slice(h * DH, (h + 1) * DH)
            l1, l2, l3 = pieces((lse_ref[i, h : h + 1, :] + SHIFT) * LOG2E)
            d1, d2, d3 = pieces(jnp.sum(prod[hs], axis=0, keepdims=True))
            aux = jnp.where(place == 6, 1.0, 0.0)
            for n, piece in enumerate((l1, l2, l3, d1, d2, d3)):
                aux = jnp.where(place == n, piece, aux)
            sx[h, i, 0:32] = qt[hs].astype(bf16)
            sx[h, i, 32:64] = dt[hs].astype(bf16)
            sx[h, i, 64:80] = aux.astype(bf16)
        return carry

    lax.fori_loop(0, NR, prep_x, 0)

    def piece_on(hf, step, xx, to_right=True, to_left=True):
        out = []
        for go, zz, s_sem, r_sem, row in (
            (to_right, (z + NZ - step) % NZ, fr_s, fr_r, right),
            (to_left, (z + step) % NZ, fl_s, fl_r, left),
        ):
            if go:
                part = er.at[hf, zz, aligned(xx * 64, 64)]
                cp = remote(part, part, s_sem.at[hf, step, xx], r_sem.at[hf, step, xx], row, b)
                cp.start()
                out.append(cp)
        done.extend(out)
        return out

    def ring(hf, step, before):
        if step < 3:
            out = []
            for n, xx in enumerate((xh, 1 - xh)):
                arrived(before[n])
                out.append(piece_on(hf, step, xx))
            return out
        for pair in before:
            arrived(pair)
        return [piece_on(hf, 3, 0, to_left=False), piece_on(hf, 3, 1, to_right=False)]

    def arrived(pair):
        for cp in pair:
            cp.wait_recv()

    w_copies, c_copies = [], []

    def pass_y(d):
        if d == 0:
            y_own.wait()
        else:
            y_copies[2 * d].wait_recv()
        y_copies[2 * d + 1].wait_recv()
        part = yr.at[((y + NY - d) % NY) * 2 + xl]
        cp = remote(part, part, w_s.at[d], w_r.at[d], r, y * 2 + (1 - xl))
        cp.start()
        w_copies.append(cp)

    def pass_x(d):
        if d == 0:
            x_own.wait()
        else:
            x_copies[d].wait_recv()
        part = xr.at[rows, 32:112, aligned(((y + NY - d) % NY) * QB, QB)]
        cp = remote(part, part, c_s.at[d], c_r.at[d], other, b)
        cp.start()
        c_copies.append(cp)

    for cp in e_copies[:3]:
        cp.wait_recv()
    e_own.wait()
    first = [piece_on(0, 0, xh)]
    for cp in e_copies[3:]:
        cp.wait_recv()
    first.append(piece_on(0, 0, 1 - xh))
    second = ring(1, 0, ((), ()))
    x_copies = {}
    for d in (1, 3, 2):
        yy = (y + d) % NY
        cp = remote(sx.at[yy], xr.at[rows, 32:112, lanes], x_s.at[d], x_r.at[d], r, yy * 2 + xl)
        cp.start()
        x_copies[d] = cp
    x_own = pltpu.make_async_copy(sx.at[y], xr.at[rows, 32:112, lanes], loc.at[1])
    x_own.start()

    for zz in range(NZ):
        m = mask_ref[:, zz * QB : (zz + 1) * QB]
        m0 = jnp.concatenate([m[:, 0:64], m[:, 128:192]], 1)
        m1 = jnp.concatenate([m[:, 64:128], m[:, 192:256]], 1)
        neg[zz] = jnp.where(jnp.where(c == 0, m0, m1) == 1, 0.0, NEG)

    def blank(i, carry):
        xr[i, 112:128, :] = jnp.zeros((16, NJ), bf16)
        return carry

    lax.fori_loop(0, 2 * NR, blank, 0)

    spot = lax.broadcasted_iota(jnp.int32, (32, KB), 0)
    zero = jnp.zeros((32, KB), bf16)
    aux_d = jnp.where((spot >= 3) & (spot < 6), -1.0, 0.0).astype(bf16)

    def left_operands(zz):
        aux_t = jnp.where(spot < 3, -1.0, jnp.where(spot == 6, neg[zz], 0.0)).astype(bf16)

        def left_operand(i, carry):
            both = yr[zz, i]
            scaled = both[0:32].astype(f32) * (SCALE * LOG2E)
            high = scaled.astype(bf16)
            low = (scaled - high.astype(f32)).astype(bf16)
            lhs_t = jnp.concatenate([high, low, zero, aux_t], 0)
            lhs_d = jnp.concatenate([zero, zero, both[32:64], aux_d], 0)
            lt[zz, i] = jnp.concatenate([lhs_t, lhs_d], 1).T
            return carry

        lax.fori_loop(0, 2 * NR, left_operand, 0)

    def source(d):
        return (y + NY - d) % NY

    pass_y(0)
    pass_x(0)
    left_operands(y * 2 + xl)
    first = ring(0, 1, first)
    second = ring(1, 1, second)
    pass_y(1)
    pass_y(3)
    left_operands(source(1) * 2 + xl)
    first = ring(0, 2, first)
    second = ring(1, 2, second)
    pass_y(2)
    left_operands(source(3) * 2 + xl)
    left_operands(source(2) * 2 + xl)
    pass_x(1)
    pass_x(3)
    w_copies[0].wait_recv()
    left_operands(source(0) * 2 + (1 - xl))
    first = ring(0, 3, first)
    second = ring(1, 3, second)
    pass_x(2)
    for n, d in ((1, 1), (2, 3), (3, 2)):
        w_copies[n].wait_recv()
        left_operands(source(d) * 2 + (1 - xl))
    for cp in c_copies:
        cp.wait_recv()

    def twice(i, carry):
        xr[i, 0:32, :] = xr[i, 32:64, :]
        return carry

    lax.fori_loop(0, 2 * NR, twice, 0)
    for pair in first:
        arrived(pair)
    blocks = [((z + 4 - m) % NZ, (z + 4 + m) % NZ if m else z) for m in range(4)]

    last = (((1,), (1,)), ((), ()))

    def score_rows(hf, m, z_a, z_b):
        gb[...] = jnp.zeros_like(gb)

        def one_row(i, carry):
            kt = jnp.concatenate([yr[z_a, i, 0:32], yr[z_b, i, 0:32]], 1)
            x = xr[i, :, hf * HJ : (hf + 1) * HJ]
            left = jnp.concatenate([lt[z_a, i], lt[z_b, i]], 0)
            td = jnp.dot(left, x, preferred_element_type=f32)
            e = jnp.concatenate([er[hf, z_a], er[hf, z_b]], 0).astype(f32)
            p = jnp.exp2(jnp.concatenate([td[0:KB], td[2 * KB : 3 * KB]], 0)) * e
            ds = p * jnp.concatenate([td[KB : 2 * KB], td[3 * KB :]], 0)
            gb[...] += ds
            pb, db = p.astype(bf16), ds.astype(bf16)
            gv = lax.dot_general(x[64:96], pb, last, preferred_element_type=f32)
            gk = lax.dot_general(x[0:32], db, last, preferred_element_type=f32)
            gq = jnp.dot(kt, db, preferred_element_type=f32)
            if m == 0:
                gqa[hf, i] = gq
            else:
                gqa[hf, i] += gq
            both = jnp.concatenate([gk * SCALE, gv], 0)
            if hf == 0:
                gka[m, i] = both
            else:
                out = (gka[m, i] + both).astype(bf16)
                sg[m, 0, i] = out[:, :KB]
                sg[m, 1, i] = out[:, KB:]
            return carry

        lax.fori_loop(0, 2 * NR, one_row, 0, unroll=2)

    def send_or_keep(is_self, src, dst, s_sem, r_sem, row, key):
        @pl.when(jnp.logical_not(is_self))
        def _():
            remote(src, dst, s_sem, r_sem, row, key).start()

        @pl.when(is_self)
        def _():
            cp = pltpu.make_async_copy(src, dst, loc.at[3])
            cp.start()
            cp.wait()

        later.append((is_self, src, dst, s_sem, r_sem, row, key))

    later = []

    parts = [(half, cc) for half in range(2) for cc in range(2)]

    def keys_part(ref, m, half, cc):
        return ref.at[m, half, cc * NR : (cc + 1) * NR]

    def keys_aside(m, half, cc):
        return remote(
            keys_part(sg, m, half, cc), keys_part(pr, m, half, cc),
            p_s.at[m, half, cc], p_r.at[m, half, cc], r, y * 2 + (1 - xl),
        )

    def keys_home(m, half, cc):
        src, dst = keys_part(sg, m, half, cc), gkvr.at[y * 2 + c]
        zz = blocks[m][half]
        return (
            (zz == b) & (c == cc), src, dst,
            g_s.at[m, half, cc], g_r.at[y * 2 + c], row_of(z, xh, cc), zz,
        )

    def return_aside(m):
        @pl.when(xl != (z + m) % 2)
        def _():
            for half, cc in parts:
                keys_aside(m, half, cc).start()

    def return_home(m):
        @pl.when(xl == (z + m) % 2)
        def _():
            for half, cc in parts:
                keys_aside(m, half, cc).wait_recv()
                at = slice(cc * NR, (cc + 1) * NR)
                total = sg[m, half, at].astype(f32) + pr[m, half, at].astype(f32)
                sg[m, half, at] = total.astype(bf16)
                is_self, *copy = keys_home(m, half, cc)

                @pl.when(jnp.logical_not(is_self))
                def _(copy=copy):
                    remote(*copy).start()

                @pl.when(is_self)
                def _(copy=copy):
                    cp = pltpu.make_async_copy(copy[0], copy[1], loc.at[3])
                    cp.start()
                    cp.wait()

    def return_drain(m):
        @pl.when(xl != (z + m) % 2)
        def _():
            for half, cc in parts:
                keys_aside(m, half, cc).wait_send()

        @pl.when(xl == (z + m) % 2)
        def _():
            for half, cc in parts:
                is_self, *copy = keys_home(m, half, cc)

                @pl.when(jnp.logical_not(is_self))
                def _(copy=copy):
                    remote(*copy).wait_send()

    def reduce_step(hf, m, before):
        if m == 0:
            own[hf] = gb[KB:, :]
            sr[hf, 0, 0:64] = gb[0:64, :].astype(bf16)
            sl[hf, 0, 64:128] = gb[64:128, :].astype(bf16)
            pick_r, pick_l = (hf, 0, slice(0, 64)), (hf, 0, slice(64, 128))
        else:
            arrived(before)
            if m == 1:
                sr[hf, m, 0:64] = (gb[0:64, :] + rr[hf, 0, 0:64].astype(f32)).astype(bf16)
                sr[hf, m, 64:128] = gb[64:128, :].astype(bf16)
                sl[hf, m, 0:64] = gb[128:192, :].astype(bf16)
                sl[hf, m, 64:128] = (gb[192:256, :] + rl[hf, 0, 64:128].astype(f32)).astype(bf16)
            else:
                sr[hf, m] = (gb[0:KB, :] + rr[hf, m - 1].astype(f32)).astype(bf16)
                sl[hf, m] = (gb[KB:, :] + rl[hf, m - 1].astype(f32)).astype(bf16)
            pick_r = pick_l = (hf, m)
        cr = remote(sr.at[pick_r], rr.at[pick_r], rr_s.at[hf, m], rr_r.at[hf, m], right, b)
        cl = remote(sl.at[pick_l], rl.at[pick_l], rl_s.at[hf, m], rl_r.at[hf, m], left, b)
        cr.start()
        cl.start()
        done.extend((cr, cl))
        return cr, cl

    theirs = pl.ds((1 - c) * NR, NR)

    def query_across(hf):
        cp = remote(gqa.at[hf, theirs], gqc.at[hf], qc_s.at[hf], qc_r.at[hf], other, b)
        cp.start()
        done.append(cp)
        return cp

    def query_back(hf, cp):
        cp.wait_recv()

        def add_q(i, carry):
            total = ((gqa[hf, c * NR + i] + gqc[hf, i]) * SCALE).astype(bf16)
            for n in range(2):
                sgq[2 * hf + n, i] = total[:, n * QB : (n + 1) * QB]
            return carry

        lax.fori_loop(0, NR, add_q, 0)
        for n in range(2):
            yy = 2 * hf + n
            send_or_keep(
                y == yy, sgq.at[yy], gqr.at[y], qy_s.at[yy], qy_r.at[y], r, yy * 2 + xl
            )

    def bias_back(hf, pair):
        arrived(pair)
        total = own[hf] + rr[hf, 3].astype(f32) + rl[hf, 3].astype(f32)
        total = total.astype(bf16)
        for xx in range(2):
            for n in range(2):
                yy = 2 * hf + n
                sb[xx, yy] = total[xx * 64 : (xx + 1) * 64, n * QB : (n + 1) * QB]
                send_or_keep(
                    (y == yy) & (xh == xx), sb.at[xx, yy], gbr.at[y, xh],
                    b_s.at[xx, yy], b_r.at[y, xh], row_of(z, xx, c), yy * 2 + xl,
                )

    reduced = [None, None]
    order = ((0, 0), (1, 0), (0, 1), (1, 1), (0, 2), (1, 2), (0, 3), (1, 3))
    for n, (hf, m) in enumerate(order):
        score_rows(hf, m, *blocks[m])
        if hf == 1:
            return_aside(m)
        reduced[hf] = reduce_step(hf, m, reduced[hf])
        if n == 0:
            for pair in second:
                arrived(pair)
        if n in (3, 5, 7):
            return_home((n - 3) // 2)
        if n == 6:
            q_pass = query_across(0)
    q_pass_1 = query_across(1)
    query_back(0, q_pass)
    bias_back(0, reduced[0])
    query_back(1, q_pass_1)
    bias_back(1, reduced[1])
    return_home(3)

    for n in range(8):

        @pl.when(n != y * 2 + c)
        def _(n=n):
            remote(sg.at[0, 0, 0:NR], gkvr.at[n], g_s.at[0, 0, 0], g_r.at[n], r, b).wait_recv()

    for n in range(NY):

        @pl.when(n != y)
        def _(n=n):
            remote(sgq.at[0], gqr.at[n], qy_s.at[0], qy_r.at[n], r, b).wait_recv()

        for xx in range(2):

            @pl.when((n != y) | (xx != xh))
            def _(n=n, xx=xx):
                remote(sb.at[0, 0], gbr.at[n, xx], b_s.at[0, 0], b_r.at[n, xx], r, b).wait_recv()

    for m in range(4):
        return_drain(m)

    for is_self, *copy in later:

        @pl.when(jnp.logical_not(is_self))
        def _(copy=copy):
            remote(*copy).wait_send()

    done.extend((*e_copies, *w_copies, *c_copies))
    for cp in (*done, *y_copies.values(), *x_copies.values()):
        cp.wait_send()


def home(gqr, gkvr, gbr, gq_ref, gk_ref, gv_ref, gb_ref):
    gq_ref[0] = jnp.concatenate([gqr[h, 0].astype(f32) for h in range(H)], 0).T
    for cc in range(2):
        for ref, lo in ((gk_ref, 0), (gv_ref, 32)):
            heads = [
                gkvr[h * 2 + cc, 0, lo : lo + 32].astype(f32) for h in range(H)
            ]
            part = jnp.concatenate(heads, 0).T
            ref[0, cc * 64 : cc * 64 + 64] = part[0:64]
            ref[0, 128 + cc * 64 : 192 + cc * 64] = part[64:128]

    @pl.when(pl.program_id(0) == 0)
    def _():
        for h in range(H):
            gb_ref[h] = gbr[h, 0].astype(f32) + gbr[h, 1].astype(f32)


def per_device(query, key_in, value, output, dout, lse, bias, mask):
    dma = pltpu.SemaphoreType.DMA
    vmem = pl.BlockSpec(memory_space=pltpu.VMEM)
    scratch = [
        pltpu.VMEM((H, 64, QB), bf16),
        pltpu.VMEM((H, NR, 80, QB), bf16),
        pltpu.VMEM((H, 2, NR, 64, KB), bf16),
        pltpu.VMEM((2, NZ, KB, HJ), bf16),
        pltpu.VMEM((2 * NR, 128, NJ), bf16),
        pltpu.VMEM((NZ, 2 * NR, 64, KB), bf16),
        pltpu.VMEM((NZ, 1, KB), f32),
        pltpu.VMEM((NZ, 2 * NR, 2 * KB, 128), bf16),
        pltpu.VMEM((2 * KB, HJ), f32),
        pltpu.VMEM((2, KB, HJ), f32),
        pltpu.VMEM((2, 4, KB, HJ), bf16),
        pltpu.VMEM((2, 4, KB, HJ), bf16),
        pltpu.VMEM((2, 4, KB, HJ), bf16),
        pltpu.VMEM((2, 4, KB, HJ), bf16),
        pltpu.VMEM((2, 2 * NR, DH, HJ), f32),
        pltpu.VMEM((4, 2 * NR, 64, 2 * KB), f32),
        pltpu.VMEM((4, 2, 2 * NR, 64, KB), bf16),
        pltpu.VMEM((4, 2, 2 * NR, 64, KB), bf16),
        pltpu.VMEM((2, NR, DH, HJ), f32),
        pltpu.VMEM((NY, NR, DH, QB), bf16),
        pltpu.VMEM((2, NY, 64, QB), bf16),
    ]
    four, pair, ring = dma((4,)), dma((2, 4)), dma((2, 4, 2))
    sems = [
        dma((8,)), dma((8,)), four, four, four, four, dma((8,)), dma((8,)), four, four,
        ring, ring, ring, ring,
        pair, pair, pair, pair, dma((4, 2, 2)), dma((4, 2, 2)), dma((4, 2, 2)), dma((8,)), dma((2,)), dma((2,)),
        four, four, pair, dma((4, 2)), four,
    ]
    gqr, gkvr, gbr = pl.pallas_call(
        kernel,
        out_shape=[
            jax.ShapeDtypeStruct((NY, NR, DH, QB), bf16),
            jax.ShapeDtypeStruct((8, NR, 64, KB), bf16),
            jax.ShapeDtypeStruct((NY, 2, 64, QB), bf16),
        ],
        in_specs=[vmem] * 8,
        out_specs=[vmem] * 3,
        scratch_shapes=scratch + sems,
        compiler_params=pltpu.CompilerParams(
            collective_id=0, has_side_effects=True, vmem_limit_bytes=56 << 20
        ),
    )(
        query, key_in, value, output, dout,
        lse.transpose(1, 0, 2), bias.transpose(0, 2, 1), mask.reshape(1, -1),
    )
    grad = jax.ShapeDtypeStruct(query.shape, f32)
    grad_spec = pl.BlockSpec((1, QB, H * DH), lambda i: (i, 0, 0))
    gq, gk, gv, gb = pl.pallas_call(
        home,
        grid=(NR,),
        out_shape=[grad, grad, grad, jax.ShapeDtypeStruct((H, 64, QB), f32)],
        in_specs=[
            pl.BlockSpec((NY, 1, DH, QB), lambda i: (0, i, 0, 0)),
            pl.BlockSpec((8, 1, 64, KB), lambda i: (0, i, 0, 0)),
            pl.BlockSpec((NY, 2, 64, QB), lambda i: (0, 0, 0, 0)),
        ],
        out_specs=[grad_spec] * 3 + [pl.BlockSpec((H, 64, QB), lambda i: (0, 0, 0))],
    )(gqr, gkvr, gbr)
    return gq, gk, gv, gb.transpose(0, 2, 1)


def solution(mesh):
    in_specs = (
        P("row", "key", None),
        P("row", "key", None),
        P("row", "key", None),
        P("row", "key", None),
        P("row", "key", None),
        P(None, "row", "key"),
        P(None, "key", "row"),
        P(),
    )
    out_specs = (
        P("row", "key", None),
        P("row", "key", None),
        P("row", "key", None),
        P(None, "key", "row"),
    )
    return jax.shard_map(
        per_device, mesh=mesh, in_specs=in_specs, out_specs=out_specs, check_vma=False
    )
```

```python
import jax
import jax.numpy as jnp
from jax import lax
from jax.experimental import pallas as pl
from jax.experimental.pallas import tpu as pltpu
from jax.sharding import PartitionSpec as P

MESH = pl.DeviceIdType.MESH
f32, bf16 = jnp.float32, jnp.bfloat16

H, DH, NR = 4, 32, 5
QB = 256
NY, NZ = 4, 8
NJ = NY * QB
HJ = NJ // 2
KB = 128
SHIFT = 6.0
LOG2E = 1.4426950408889634
SCALE = DH**-0.5
NEG = -1e30


def pieces(a):
    first = a.astype(bf16).astype(f32)
    rest = a - first
    second = rest.astype(bf16).astype(f32)
    return first, second, rest - second


def aligned(start, size):
    return pl.ds(pl.multiple_of(start, size), size)


def kernel(
    q_ref, k_ref, v_ref, o_ref, do_ref, lse_ref, bias_ref, mask_ref,
    gqr, gkvr, gbr,
    se, sx, sy, er, xr, yr, neg, lt, gb, sr, sl, rr, rl, gqa, gka, sg, pr, gqc, sgq, sb,
    e_s, e_r, x_s, x_r, c_s, c_r, y_s, y_r, w_s, w_r, fr_s, fr_r, fl_s, fl_r,
    rr_s, rr_r, rl_s, rl_r, p_s, p_r, g_s, g_r, qc_s, qc_r, qy_s, qy_r, b_s, b_r, loc,
):
    r, b = lax.axis_index("row"), lax.axis_index("key")
    z, xh, c = r // 4, (r // 2) % 2, r % 2
    y, xl = b // 2, b % 2

    def row_of(zz, xx, cc):
        return zz * 4 + xx * 2 + cc

    def remote(src, dst, s_sem, r_sem, row, key):
        return pltpu.make_async_remote_copy(
            src_ref=src, dst_ref=dst, send_sem=s_sem, recv_sem=r_sem,
            device_id=(row, key), device_id_type=MESH,
        )

    right = row_of((z + 1) % NZ, xh, c)
    left = row_of((z + NZ - 1) % NZ, xh, c)
    across = row_of(z, 1 - xh, c)
    other = row_of(z, xh, 1 - c)
    done = []

    barrier = pltpu.get_barrier_semaphore()
    greet = [(right, b), (left, b)]
    greet += [(across, ((y + d) % NY) * 2 + xl) for d in range(NY)]
    greet += [
        (row_of(z, xh, c ^ ((n // 2) % 2)), ((y + n // 4) % NY) * 2 + (xl ^ (n % 2)))
        for n in range(1, 16)
    ]
    for device in greet:
        pl.semaphore_signal(barrier, inc=1, device_id=device, device_id_type=MESH)

    for h in range(H):
        se[h] = jnp.exp(bias_ref[h] + SHIFT).astype(bf16)

    pl.semaphore_wait(barrier, len(greet))

    mine = aligned(xh * 64, 64)
    lanes = aligned(y * QB, QB)
    lanes_e = aligned((y % 2) * QB, QB)
    rows = pl.ds(c * NR, NR)

    e_place = er.at[y // 2, z, mine, lanes_e]
    e_copies = []
    for n in (1, 3, 2, 4, 5, 7, 6):
        yy = (y + n % 4) % NY
        cp = remote(
            se.at[yy], e_place, e_s.at[n], e_r.at[n], row_of(z, xh ^ (n // 4), c), yy * 2 + xl
        )
        cp.start()
        e_copies.append(cp)
    e_own = pltpu.make_async_copy(se.at[y], e_place, loc.at[0])
    e_own.start()

    def prep_y(i, carry):
        for ref, lo in ((k_ref, 0), (v_ref, 32)):
            full = ref[i].astype(f32)
            for cc in range(2):
                part = jnp.concatenate(
                    [full[cc * 64 : cc * 64 + 64], full[128 + cc * 64 : 192 + cc * 64]], 0
                ).T
                for h in range(H):
                    sy[h, cc, i, lo : lo + 32] = part[h * DH : (h + 1) * DH].astype(bf16)
        return carry

    lax.fori_loop(0, NR, prep_y, 0)

    y_copies = {}
    for n in (1, 2, 3, 6, 7, 4, 5):
        d, dc = n // 2, n % 2
        yy, cc = (y + d) % NY, c ^ dc
        cp = remote(
            sy.at[yy, cc], yr.at[b, rows], y_s.at[n], y_r.at[n], row_of(z, xh, cc), yy * 2 + xl
        )
        cp.start()
        y_copies[n] = cp
    y_own = pltpu.make_async_copy(sy.at[y, c], yr.at[b, rows], loc.at[2])
    y_own.start()

    place = lax.broadcasted_iota(jnp.int32, (16, QB), 0)

    def prep_x(i, carry):
        qt = q_ref[i].astype(f32).T
        d_out = do_ref[i].astype(f32)
        dt = d_out.T
        prod = (d_out * o_ref[i].astype(f32)).T
        for h in range(H):
            hs = slice(h * DH, (h + 1) * DH)
            l1, l2, l3 = pieces((lse_ref[i, h : h + 1, :] + SHIFT) * LOG2E)
            d1, d2, d3 = pieces(jnp.sum(prod[hs], axis=0, keepdims=True))
            aux = jnp.where(place == 6, 1.0, 0.0)
            for n, piece in enumerate((l1, l2, l3, d1, d2, d3)):
                aux = jnp.where(place == n, piece, aux)
            sx[h, i, 0:32] = qt[hs].astype(bf16)
            sx[h, i, 32:64] = dt[hs].astype(bf16)
            sx[h, i, 64:80] = aux.astype(bf16)
        return carry

    lax.fori_loop(0, NR, prep_x, 0)

    def piece_on(hf, step, xx, to_right=True, to_left=True):
        out = []
        for go, zz, s_sem, r_sem, row in (
            (to_right, (z + NZ - step) % NZ, fr_s, fr_r, right),
            (to_left, (z + step) % NZ, fl_s, fl_r, left),
        ):
            if go:
                part = er.at[hf, zz, aligned(xx * 64, 64)]
                cp = remote(part, part, s_sem.at[hf, step, xx], r_sem.at[hf, step, xx], row, b)
                cp.start()
                out.append(cp)
        done.extend(out)
        return out

    def ring(hf, step, before):
        if step < 3:
            out = []
            for n, xx in enumerate((xh, 1 - xh)):
                arrived(before[n])
                out.append(piece_on(hf, step, xx))
            return out
        for pair in before:
            arrived(pair)
        return [piece_on(hf, 3, 0, to_left=False), piece_on(hf, 3, 1, to_right=False)]

    def arrived(pair):
        for cp in pair:
            cp.wait_recv()

    w_copies, c_copies = [], []

    def pass_y(d):
        if d == 0:
            y_own.wait()
        else:
            y_copies[2 * d].wait_recv()
        y_copies[2 * d + 1].wait_recv()
        part = yr.at[((y + NY - d) % NY) * 2 + xl]
        cp = remote(part, part, w_s.at[d], w_r.at[d], r, y * 2 + (1 - xl))
        cp.start()
        w_copies.append(cp)

    def pass_x(d):
        if d == 0:
            x_own.wait()
        else:
            x_copies[d].wait_recv()
        part = xr.at[rows, 32:112, aligned(((y + NY - d) % NY) * QB, QB)]
        cp = remote(part, part, c_s.at[d], c_r.at[d], other, b)
        cp.start()
        c_copies.append(cp)

    for cp in e_copies[:3]:
        cp.wait_recv()
    e_own.wait()
    first = [piece_on(0, 0, xh)]
    for cp in e_copies[3:]:
        cp.wait_recv()
    first.append(piece_on(0, 0, 1 - xh))
    second = ring(1, 0, ((), ()))
    x_copies = {}
    for d in (1, 3, 2):
        yy = (y + d) % NY
        cp = remote(sx.at[yy], xr.at[rows, 32:112, lanes], x_s.at[d], x_r.at[d], r, yy * 2 + xl)
        cp.start()
        x_copies[d] = cp
    x_own = pltpu.make_async_copy(sx.at[y], xr.at[rows, 32:112, lanes], loc.at[1])
    x_own.start()

    for zz in range(NZ):
        m = mask_ref[:, zz * QB : (zz + 1) * QB]
        m0 = jnp.concatenate([m[:, 0:64], m[:, 128:192]], 1)
        m1 = jnp.concatenate([m[:, 64:128], m[:, 192:256]], 1)
        neg[zz] = jnp.where(jnp.where(c == 0, m0, m1) == 1, 0.0, NEG)

    def blank(i, carry):
        xr[i, 112:128, :] = jnp.zeros((16, NJ), bf16)
        return carry

    lax.fori_loop(0, 2 * NR, blank, 0)

    spot = lax.broadcasted_iota(jnp.int32, (32, KB), 0)
    zero = jnp.zeros((32, KB), bf16)
    aux_d = jnp.where((spot >= 3) & (spot < 6), -1.0, 0.0).astype(bf16)

    def left_operands(zz):
        aux_t = jnp.where(spot < 3, -1.0, jnp.where(spot == 6, neg[zz], 0.0)).astype(bf16)

        def left_operand(i, carry):
            both = yr[zz, i]
            scaled = both[0:32].astype(f32) * (SCALE * LOG2E)
            high = scaled.astype(bf16)
            low = (scaled - high.astype(f32)).astype(bf16)
            lhs_t = jnp.concatenate([high, low, zero, aux_t], 0)
            lhs_d = jnp.concatenate([zero, zero, both[32:64], aux_d], 0)
            lt[zz, i] = jnp.concatenate([lhs_t, lhs_d], 1).T
            return carry

        lax.fori_loop(0, 2 * NR, left_operand, 0)

    def source(d):
        return (y + NY - d) % NY

    pass_y(0)
    pass_x(0)
    left_operands(y * 2 + xl)
    first = ring(0, 1, first)
    second = ring(1, 1, second)
    pass_y(1)
    pass_y(3)
    left_operands(source(1) * 2 + xl)
    first = ring(0, 2, first)
    pass_y(2)
    second = ring(1, 2, second)
    left_operands(source(3) * 2 + xl)
    left_operands(source(2) * 2 + xl)
    pass_x(1)
    pass_x(3)
    w_copies[0].wait_recv()
    left_operands(source(0) * 2 + (1 - xl))
    first = ring(0, 3, first)
    pass_x(2)
    for n, d in ((1, 1), (2, 3), (3, 2)):
        w_copies[n].wait_recv()
        left_operands(source(d) * 2 + (1 - xl))
    for cp in c_copies:
        cp.wait_recv()

    def twice(i, carry):
        xr[i, 0:32, :] = xr[i, 32:64, :]
        return carry

    lax.fori_loop(0, 2 * NR, twice, 0)
    blocks = [((z + 4 - m) % NZ, (z + 4 + m) % NZ if m else z) for m in range(4)]

    last = (((1,), (1,)), ((), ()))

    def score_rows(hf, m, z_a, z_b):
        gb[hf, m] = jnp.zeros((2 * KB, HJ), f32)

        def one_row(i, carry):
            kt = jnp.concatenate([yr[z_a, i, 0:32], yr[z_b, i, 0:32]], 1)
            x = xr[i, :, hf * HJ : (hf + 1) * HJ]
            left = jnp.concatenate([lt[z_a, i], lt[z_b, i]], 0)
            td = jnp.dot(left, x, preferred_element_type=f32)
            e = jnp.concatenate([er[hf, z_a], er[hf, z_b]], 0).astype(f32)
            p = jnp.exp2(jnp.concatenate([td[0:KB], td[2 * KB : 3 * KB]], 0)) * e
            ds = p * jnp.concatenate([td[KB : 2 * KB], td[3 * KB :]], 0)
            gb[hf, m] += ds
            pb, db = p.astype(bf16), ds.astype(bf16)
            gv = lax.dot_general(x[64:96], pb, last, preferred_element_type=f32)
            gk = lax.dot_general(x[0:32], db, last, preferred_element_type=f32)
            gq = jnp.dot(kt, db, preferred_element_type=f32)
            if m == 1:
                gqa[hf, i] = gq
            else:
                gqa[hf, i] += gq
            both = jnp.concatenate([gk * SCALE, gv], 0)
            if hf == 0:
                gka[m, i] = both
            else:
                out = (gka[m, i] + both).astype(bf16)
                sg[m, 0, i] = out[:, :KB]
                sg[m, 1, i] = out[:, KB:]
            return carry

        lax.fori_loop(0, 2 * NR, one_row, 0, unroll=2 * NR)

    def send_or_keep(is_self, src, dst, s_sem, r_sem, row, key):
        @pl.when(jnp.logical_not(is_self))
        def _():
            remote(src, dst, s_sem, r_sem, row, key).start()

        @pl.when(is_self)
        def _():
            cp = pltpu.make_async_copy(src, dst, loc.at[3])
            cp.start()
            cp.wait()

        later.append((is_self, src, dst, s_sem, r_sem, row, key))

    later = []

    parts = [(half, cc) for half in range(2) for cc in range(2)]

    def keys_part(ref, m, half, cc):
        return ref.at[m, half, cc * NR : (cc + 1) * NR]

    def keys_aside(m, half, cc):
        return remote(
            keys_part(sg, m, half, cc), keys_part(pr, m, half, cc),
            p_s.at[m, half, cc], p_r.at[m, half, cc], r, y * 2 + (1 - xl),
        )

    def keys_home(m, half, cc):
        src, dst = keys_part(sg, m, half, cc), gkvr.at[y * 2 + c]
        zz = blocks[m][half]
        return (
            (zz == b) & (c == cc), src, dst,
            g_s.at[m, half, cc], g_r.at[y * 2 + c], row_of(z, xh, cc), zz,
        )

    def return_aside(m):
        @pl.when(xl != (z + m) % 2)
        def _():
            for half, cc in parts:
                keys_aside(m, half, cc).start()

    def return_home(m):
        @pl.when(xl == (z + m) % 2)
        def _():
            for half, cc in parts:
                keys_aside(m, half, cc).wait_recv()
                at = slice(cc * NR, (cc + 1) * NR)
                total = sg[m, half, at].astype(f32) + pr[m, half, at].astype(f32)
                sg[m, half, at] = total.astype(bf16)
                is_self, *copy = keys_home(m, half, cc)

                @pl.when(jnp.logical_not(is_self))
                def _(copy=copy):
                    remote(*copy).start()

                @pl.when(is_self)
                def _(copy=copy):
                    cp = pltpu.make_async_copy(copy[0], copy[1], loc.at[3])
                    cp.start()
                    cp.wait()

    def return_drain(m):
        @pl.when(xl != (z + m) % 2)
        def _():
            for half, cc in parts:
                keys_aside(m, half, cc).wait_send()

        @pl.when(xl == (z + m) % 2)
        def _():
            for half, cc in parts:
                is_self, *copy = keys_home(m, half, cc)

                @pl.when(jnp.logical_not(is_self))
                def _(copy=copy):
                    remote(*copy).wait_send()

    def reduce_step(hf, m, before):
        low, high = slice(0, 64), slice(64, KB)
        if m == 0:
            sr[hf, 0, low] = gb[hf, 0, 0:64].astype(bf16)
            sl[hf, 0, high] = gb[hf, 0, 64:128].astype(bf16)
            pick_r, pick_l = (hf, 0, low), (hf, 0, high)
        else:
            arrived(before)
            if m == 1:
                sr[hf, m, low] = (gb[hf, m, 0:64] + rr[hf, 0, low].astype(f32)).astype(bf16)
                sr[hf, m, high] = gb[hf, m, 64:128].astype(bf16)
                sl[hf, m, low] = gb[hf, m, 128:192].astype(bf16)
                sl[hf, m, high] = (gb[hf, m, 192:256] + rl[hf, 0, high].astype(f32)).astype(bf16)
            else:
                sr[hf, m] = (gb[hf, m, 0:KB] + rr[hf, m - 1].astype(f32)).astype(bf16)
                sl[hf, m] = (gb[hf, m, KB:] + rl[hf, m - 1].astype(f32)).astype(bf16)
            pick_r = pick_l = (hf, m)
        cr = remote(sr.at[pick_r], rr.at[pick_r], rr_s.at[hf, m], rr_r.at[hf, m], right, b)
        cl = remote(sl.at[pick_l], rl.at[pick_l], rl_s.at[hf, m], rl_r.at[hf, m], left, b)
        cr.start()
        cl.start()
        done.extend((cr, cl))
        return cr, cl

    theirs = pl.ds((1 - c) * NR, NR)

    def query_across(hf):
        cp = remote(gqa.at[hf, theirs], gqc.at[hf], qc_s.at[hf], qc_r.at[hf], other, b)
        cp.start()
        done.append(cp)
        return cp

    def query_back(hf, cp):
        cp.wait_recv()

        def add_q(i, carry):
            total = ((gqa[hf, c * NR + i] + gqc[hf, i]) * SCALE).astype(bf16)
            for n in range(2):
                sgq[2 * hf + n, i] = total[:, n * QB : (n + 1) * QB]
            return carry

        lax.fori_loop(0, NR, add_q, 0)
        for n in range(2):
            yy = 2 * hf + n
            send_or_keep(
                y == yy, sgq.at[yy], gqr.at[y], qy_s.at[yy], qy_r.at[y], r, yy * 2 + xl
            )

    def bias_back(hf, pair):
        arrived(pair)
        total = gb[hf, 0, KB:] + rr[hf, 3].astype(f32) + rl[hf, 3].astype(f32)
        total = total.astype(bf16)
        for xx in range(2):
            for n in range(2):
                yy = 2 * hf + n
                sb[xx, yy] = total[xx * 64 : (xx + 1) * 64, n * QB : (n + 1) * QB]
                send_or_keep(
                    (y == yy) & (xh == xx), sb.at[xx, yy], gbr.at[y, xh],
                    b_s.at[xx, yy], b_r.at[y, xh], row_of(z, xx, c), yy * 2 + xl,
                )

    order = ((0, 1), (1, 1), (0, 0), (1, 0), (0, 2), (1, 2), (0, 3), (1, 3))
    sums = {2: ((0, 0),), 3: ((1, 0), (0, 1)), 4: ((1, 1),), 5: ((0, 2),), 6: ((1, 2), (0, 3)), 7: ((1, 3),)}
    reduced = [None, None]
    for n, (hf, m) in enumerate(order):
        score_rows(hf, m, *blocks[m])
        if hf == 1:
            return_aside(m)
        for part in sums.get(n, ()):
            reduced[part[0]] = reduce_step(*part, reduced[part[0]])
        if n == 0:
            second = ring(1, 3, second)
        if n == 1:
            for pair in first:
                arrived(pair)
        if n == 2:
            for pair in second:
                arrived(pair)
        if n == 4:
            return_home(1)
        if n == 6:
            return_home(0)
            q_pass = query_across(0)
    q_pass_1 = query_across(1)
    return_home(2)
    query_back(0, q_pass)
    query_back(1, q_pass_1)
    bias_back(0, reduced[0])
    bias_back(1, reduced[1])
    return_home(3)

    for n in range(8):

        @pl.when(n != y * 2 + c)
        def _(n=n):
            remote(sg.at[0, 0, 0:NR], gkvr.at[n], g_s.at[0, 0, 0], g_r.at[n], r, b).wait_recv()

    for n in range(NY):

        @pl.when(n != y)
        def _(n=n):
            remote(sgq.at[0], gqr.at[n], qy_s.at[0], qy_r.at[n], r, b).wait_recv()

        for xx in range(2):

            @pl.when((n != y) | (xx != xh))
            def _(n=n, xx=xx):
                remote(sb.at[0, 0], gbr.at[n, xx], b_s.at[0, 0], b_r.at[n, xx], r, b).wait_recv()

    for m in range(4):
        return_drain(m)

    for is_self, *copy in later:

        @pl.when(jnp.logical_not(is_self))
        def _(copy=copy):
            remote(*copy).wait_send()

    done.extend((*e_copies, *w_copies, *c_copies))
    for cp in (*done, *y_copies.values(), *x_copies.values()):
        cp.wait_send()


def home(gqr, gkvr, gbr, gq_ref, gk_ref, gv_ref, gb_ref):
    for i in range(NR):
        gq_ref[i] = jnp.concatenate([gqr[h, i].astype(f32) for h in range(H)], 0).T
        for cc in range(2):
            for ref, lo in ((gk_ref, 0), (gv_ref, 32)):
                heads = [gkvr[h * 2 + cc, i, lo : lo + 32].astype(f32) for h in range(H)]
                part = jnp.concatenate(heads, 0).T
                ref[i, cc * 64 : cc * 64 + 64] = part[0:64]
                ref[i, 128 + cc * 64 : 192 + cc * 64] = part[64:128]
    for h in range(H):
        gb_ref[h] = gbr[h, 0].astype(f32) + gbr[h, 1].astype(f32)


def per_device(query, key_in, value, output, dout, lse, bias, mask):
    dma = pltpu.SemaphoreType.DMA
    vmem = pl.BlockSpec(memory_space=pltpu.VMEM)
    scratch = [
        pltpu.VMEM((H, 64, QB), bf16),
        pltpu.VMEM((H, NR, 80, QB), bf16),
        pltpu.VMEM((H, 2, NR, 64, KB), bf16),
        pltpu.VMEM((2, NZ, KB, HJ), bf16),
        pltpu.VMEM((2 * NR, 128, NJ), bf16),
        pltpu.VMEM((NZ, 2 * NR, 64, KB), bf16),
        pltpu.VMEM((NZ, 1, KB), f32),
        pltpu.VMEM((NZ, 2 * NR, 2 * KB, 128), bf16),
        pltpu.VMEM((2, 4, 2 * KB, HJ), f32),
        pltpu.VMEM((2, 4, KB, HJ), bf16),
        pltpu.VMEM((2, 4, KB, HJ), bf16),
        pltpu.VMEM((2, 4, KB, HJ), bf16),
        pltpu.VMEM((2, 4, KB, HJ), bf16),
        pltpu.VMEM((2, 2 * NR, DH, HJ), f32),
        pltpu.VMEM((4, 2 * NR, 64, 2 * KB), f32),
        pltpu.VMEM((4, 2, 2 * NR, 64, KB), bf16),
        pltpu.VMEM((4, 2, 2 * NR, 64, KB), bf16),
        pltpu.VMEM((2, NR, DH, HJ), f32),
        pltpu.VMEM((NY, NR, DH, QB), bf16),
        pltpu.VMEM((2, NY, 64, QB), bf16),
    ]
    four, pair, ring = dma((4,)), dma((2, 4)), dma((2, 4, 2))
    sems = [
        dma((8,)), dma((8,)), four, four, four, four, dma((8,)), dma((8,)), four, four,
        ring, ring, ring, ring,
        pair, pair, pair, pair, dma((4, 2, 2)), dma((4, 2, 2)), dma((4, 2, 2)), dma((8,)), dma((2,)), dma((2,)),
        four, four, pair, dma((4, 2)), four,
    ]
    gqr, gkvr, gbr = pl.pallas_call(
        kernel,
        out_shape=[
            jax.ShapeDtypeStruct((NY, NR, DH, QB), bf16),
            jax.ShapeDtypeStruct((8, NR, 64, KB), bf16),
            jax.ShapeDtypeStruct((NY, 2, 64, QB), bf16),
        ],
        in_specs=[vmem] * 8,
        out_specs=[vmem] * 3,
        scratch_shapes=scratch + sems,
        compiler_params=pltpu.CompilerParams(
            collective_id=0, has_side_effects=True, vmem_limit_bytes=56 << 20
        ),
    )(
        query, key_in, value, output, dout,
        lse.transpose(1, 0, 2), bias.transpose(0, 2, 1), mask.reshape(1, -1),
    )
    grad = jax.ShapeDtypeStruct(query.shape, f32)
    gq, gk, gv, gb = pl.pallas_call(
        home,
        out_shape=[grad, grad, grad, jax.ShapeDtypeStruct((H, 64, QB), f32)],
        in_specs=[vmem] * 3,
        out_specs=[vmem] * 4,
    )(gqr, gkvr, gbr)
    return gq, gk, gv, gb.transpose(0, 2, 1)


def solution(mesh):
    in_specs = (
        P("row", "key", None),
        P("row", "key", None),
        P("row", "key", None),
        P("row", "key", None),
        P("row", "key", None),
        P(None, "row", "key"),
        P(None, "key", "row"),
        P(),
    )
    out_specs = (
        P("row", "key", None),
        P("row", "key", None),
        P("row", "key", None),
        P(None, "key", "row"),
    )
    return jax.shard_map(
        per_device, mesh=mesh, in_specs=in_specs, out_specs=out_specs, check_vma=False
    )
```

```python
import jax
import jax.numpy as jnp
from jax import lax
from jax.experimental import pallas as pl
from jax.experimental.pallas import tpu as pltpu
from jax.sharding import PartitionSpec as P

MESH = pl.DeviceIdType.MESH
f32, bf16 = jnp.float32, jnp.bfloat16

H, DH, NR = 4, 32, 5
QB = 256
NY, NZ = 4, 8
NJ = NY * QB
HJ = NJ // 2
KB = 128
SHIFT = 6.0
LOG2E = 1.4426950408889634
SCALE = DH**-0.5
NEG = -1e30


def pieces(a):
    first = a.astype(bf16).astype(f32)
    rest = a - first
    second = rest.astype(bf16).astype(f32)
    return first, second, rest - second


def aligned(start, size):
    return pl.ds(pl.multiple_of(start, size), size)


def kernel(
    q_ref, k_ref, v_ref, o_ref, do_ref, lse_ref, bias_ref, mask_ref,
    gqr, gkvr, gbr,
    se, sx, sy, er, xr, yr, neg, lt, gb, sr, sl, rr, rl, gqa, gka, sg, pr, gqc, sgq, sb,
    e_s, e_r, x_s, x_r, c_s, c_r, y_s, y_r, w_s, w_r, fr_s, fr_r, fl_s, fl_r,
    rr_s, rr_r, rl_s, rl_r, p_s, p_r, g_s, g_r, qc_s, qc_r, qy_s, qy_r, b_s, b_r, loc,
):
    r, b = lax.axis_index("row"), lax.axis_index("key")
    z, xh, c = r // 4, (r // 2) % 2, r % 2
    y, xl = b // 2, b % 2

    def row_of(zz, xx, cc):
        return zz * 4 + xx * 2 + cc

    def remote(src, dst, s_sem, r_sem, row, key):
        return pltpu.make_async_remote_copy(
            src_ref=src, dst_ref=dst, send_sem=s_sem, recv_sem=r_sem,
            device_id=(row, key), device_id_type=MESH,
        )

    right = row_of((z + 1) % NZ, xh, c)
    left = row_of((z + NZ - 1) % NZ, xh, c)
    across = row_of(z, 1 - xh, c)
    other = row_of(z, xh, 1 - c)
    done = []

    barrier = pltpu.get_barrier_semaphore()
    greet = [(right, b), (left, b)]
    greet += [(across, ((y + d) % NY) * 2 + xl) for d in range(NY)]
    greet += [
        (row_of(z, xh, c ^ ((n // 2) % 2)), ((y + n // 4) % NY) * 2 + (xl ^ (n % 2)))
        for n in range(1, 16)
    ]
    for device in greet:
        pl.semaphore_signal(barrier, inc=1, device_id=device, device_id_type=MESH)

    for h in range(H):
        se[h] = jnp.exp(bias_ref[h] + SHIFT).astype(bf16)

    pl.semaphore_wait(barrier, len(greet))

    mine = aligned(xh * 64, 64)
    lanes = aligned(y * QB, QB)
    lanes_e = aligned((y % 2) * QB, QB)
    rows = pl.ds(c * NR, NR)

    e_place = er.at[y // 2, z, mine, lanes_e]
    e_copies = []
    for n in (1, 3, 2, 4, 5, 7, 6):
        yy = (y + n % 4) % NY
        cp = remote(
            se.at[yy], e_place, e_s.at[n], e_r.at[n], row_of(z, xh ^ (n // 4), c), yy * 2 + xl
        )
        cp.start()
        e_copies.append(cp)
    e_own = pltpu.make_async_copy(se.at[y], e_place, loc.at[0])
    e_own.start()

    def prep_y(i, carry):
        for ref, lo in ((k_ref, 0), (v_ref, 32)):
            full = ref[i].astype(f32)
            for cc in range(2):
                part = jnp.concatenate(
                    [full[cc * 64 : cc * 64 + 64], full[128 + cc * 64 : 192 + cc * 64]], 0
                ).T
                for h in range(H):
                    sy[h, cc, i, lo : lo + 32] = part[h * DH : (h + 1) * DH].astype(bf16)
        return carry

    lax.fori_loop(0, NR, prep_y, 0)

    y_copies = {}
    for n in (1, 2, 3, 6, 7, 4, 5):
        d, dc = n // 2, n % 2
        yy, cc = (y + d) % NY, c ^ dc
        cp = remote(
            sy.at[yy, cc], yr.at[b, rows], y_s.at[n], y_r.at[n], row_of(z, xh, cc), yy * 2 + xl
        )
        cp.start()
        y_copies[n] = cp
    y_own = pltpu.make_async_copy(sy.at[y, c], yr.at[b, rows], loc.at[2])
    y_own.start()

    place = lax.broadcasted_iota(jnp.int32, (16, QB), 0)

    def prep_x(i, carry):
        qt = q_ref[i].astype(f32).T
        d_out = do_ref[i].astype(f32)
        dt = d_out.T
        prod = (d_out * o_ref[i].astype(f32)).T
        for h in range(H):
            hs = slice(h * DH, (h + 1) * DH)
            l1, l2, l3 = pieces((lse_ref[i, h : h + 1, :] + SHIFT) * LOG2E)
            d1, d2, d3 = pieces(jnp.sum(prod[hs], axis=0, keepdims=True))
            aux = jnp.where(place == 6, 1.0, 0.0)
            for n, piece in enumerate((l1, l2, l3, d1, d2, d3)):
                aux = jnp.where(place == n, piece, aux)
            sx[h, i, 0:32] = qt[hs].astype(bf16)
            sx[h, i, 32:64] = dt[hs].astype(bf16)
            sx[h, i, 64:80] = aux.astype(bf16)
        return carry

    lax.fori_loop(0, NR, prep_x, 0)

    def piece_on(hf, step, xx, to_right=True, to_left=True):
        out = []
        for go, zz, s_sem, r_sem, row in (
            (to_right, (z + NZ - step) % NZ, fr_s, fr_r, right),
            (to_left, (z + step) % NZ, fl_s, fl_r, left),
        ):
            if go:
                part = er.at[hf, zz, aligned(xx * 64, 64)]
                cp = remote(part, part, s_sem.at[hf, step, xx], r_sem.at[hf, step, xx], row, b)
                cp.start()
                out.append(cp)
        done.extend(out)
        return out

    def ring(hf, step, before):
        if step < 3:
            out = []
            for n, xx in enumerate((xh, 1 - xh)):
                arrived(before[n])
                out.append(piece_on(hf, step, xx))
            return out
        for pair in before:
            arrived(pair)
        return [piece_on(hf, 3, 0, to_left=False), piece_on(hf, 3, 1, to_right=False)]

    def arrived(pair):
        for cp in pair:
            cp.wait_recv()

    w_copies, c_copies = [], []

    def pass_y(d):
        if d == 0:
            y_own.wait()
        else:
            y_copies[2 * d].wait_recv()
        y_copies[2 * d + 1].wait_recv()
        part = yr.at[((y + NY - d) % NY) * 2 + xl]
        cp = remote(part, part, w_s.at[d], w_r.at[d], r, y * 2 + (1 - xl))
        cp.start()
        w_copies.append(cp)

    def pass_x(d):
        if d == 0:
            x_own.wait()
        else:
            x_copies[d].wait_recv()
        part = xr.at[rows, 32:112, aligned(((y + NY - d) % NY) * QB, QB)]
        cp = remote(part, part, c_s.at[d], c_r.at[d], other, b)
        cp.start()
        c_copies.append(cp)

    for cp in e_copies[:3]:
        cp.wait_recv()
    e_own.wait()
    first = [piece_on(0, 0, xh)]
    for cp in e_copies[3:]:
        cp.wait_recv()
    first.append(piece_on(0, 0, 1 - xh))
    second = ring(1, 0, ((), ()))
    x_copies = {}
    for d in (1, 3, 2):
        yy = (y + d) % NY
        cp = remote(sx.at[yy], xr.at[rows, 32:112, lanes], x_s.at[d], x_r.at[d], r, yy * 2 + xl)
        cp.start()
        x_copies[d] = cp
    x_own = pltpu.make_async_copy(sx.at[y], xr.at[rows, 32:112, lanes], loc.at[1])
    x_own.start()

    for zz in range(NZ):
        m = mask_ref[:, zz * QB : (zz + 1) * QB]
        m0 = jnp.concatenate([m[:, 0:64], m[:, 128:192]], 1)
        m1 = jnp.concatenate([m[:, 64:128], m[:, 192:256]], 1)
        neg[zz] = jnp.where(jnp.where(c == 0, m0, m1) == 1, 0.0, NEG)

    def blank(i, carry):
        xr[i, 112:128, :] = jnp.zeros((16, NJ), bf16)
        return carry

    lax.fori_loop(0, 2 * NR, blank, 0)

    spot = lax.broadcasted_iota(jnp.int32, (32, KB), 0)
    zero = jnp.zeros((32, KB), bf16)
    aux_d = jnp.where((spot >= 3) & (spot < 6), -1.0, 0.0).astype(bf16)

    def left_operands(zz):
        aux_t = jnp.where(spot < 3, -1.0, jnp.where(spot == 6, neg[zz], 0.0)).astype(bf16)

        def left_operand(i, carry):
            both = yr[zz, i]
            scaled = both[0:32].astype(f32) * (SCALE * LOG2E)
            high = scaled.astype(bf16)
            low = (scaled - high.astype(f32)).astype(bf16)
            lhs_t = jnp.concatenate([high, low, zero, aux_t], 0)
            lhs_d = jnp.concatenate([zero, zero, both[32:64], aux_d], 0)
            lt[zz, i] = jnp.concatenate([lhs_t, lhs_d], 1).T
            return carry

        lax.fori_loop(0, 2 * NR, left_operand, 0)

    def source(d):
        return (y + NY - d) % NY

    pass_y(0)
    pass_x(0)
    left_operands(y * 2 + xl)
    first = ring(0, 1, first)
    second = ring(1, 1, second)
    pass_y(1)
    pass_y(3)
    left_operands(source(1) * 2 + xl)
    first = ring(0, 2, first)
    pass_y(2)
    second = ring(1, 2, second)
    left_operands(source(3) * 2 + xl)
    left_operands(source(2) * 2 + xl)
    pass_x(1)
    pass_x(3)
    w_copies[0].wait_recv()
    left_operands(source(0) * 2 + (1 - xl))
    first = ring(0, 3, first)
    pass_x(2)
    for n, d in ((1, 1), (2, 3), (3, 2)):
        w_copies[n].wait_recv()
        left_operands(source(d) * 2 + (1 - xl))
    for cp in c_copies:
        cp.wait_recv()

    def twice(i, carry):
        xr[i, 0:32, :] = xr[i, 32:64, :]
        return carry

    lax.fori_loop(0, 2 * NR, twice, 0)
    blocks = [((z + 4 - m) % NZ, (z + 4 + m) % NZ if m else z) for m in range(4)]

    last = (((1,), (1,)), ((), ()))

    def score_rows(hf, m, z_a, z_b):
        gb[hf, m] = jnp.zeros((2 * KB, HJ), f32)

        def one_row(i, carry):
            kt = jnp.concatenate([yr[z_a, i, 0:32], yr[z_b, i, 0:32]], 1)
            x = xr[i, :, hf * HJ : (hf + 1) * HJ]
            left = jnp.concatenate([lt[z_a, i], lt[z_b, i]], 0)
            td = jnp.dot(left, x, preferred_element_type=f32)
            e = jnp.concatenate([er[hf, z_a], er[hf, z_b]], 0).astype(f32)
            p = jnp.exp2(jnp.concatenate([td[0:KB], td[2 * KB : 3 * KB]], 0)) * e
            ds = p * jnp.concatenate([td[KB : 2 * KB], td[3 * KB :]], 0)
            gb[hf, m] += ds
            pb, db = p.astype(bf16), ds.astype(bf16)
            gv = lax.dot_general(x[64:96], pb, last, preferred_element_type=f32)
            gk = lax.dot_general(x[0:32], db, last, preferred_element_type=f32)
            gq = jnp.dot(kt, db, preferred_element_type=f32)
            if m == 1:
                gqa[hf, i] = gq
            else:
                gqa[hf, i] += gq
            both = jnp.concatenate([gk * SCALE, gv], 0)
            if hf == 0:
                gka[m, i] = both
            else:
                out = (gka[m, i] + both).astype(bf16)
                sg[m, 0, i] = out[:, :KB]
                sg[m, 1, i] = out[:, KB:]
            return carry

        lax.fori_loop(0, 2 * NR, one_row, 0, unroll=2 * NR)

    def send_or_keep(is_self, src, dst, s_sem, r_sem, row, key):
        @pl.when(jnp.logical_not(is_self))
        def _():
            remote(src, dst, s_sem, r_sem, row, key).start()

        @pl.when(is_self)
        def _():
            dst[...] = src[...]

        later.append((is_self, src, dst, s_sem, r_sem, row, key))

    later = []

    parts = [(half, cc) for half in range(2) for cc in range(2)]

    def keys_part(ref, m, half, cc):
        return ref.at[m, half, cc * NR : (cc + 1) * NR]

    def keys_aside(m, half, cc):
        return remote(
            keys_part(sg, m, half, cc), keys_part(pr, m, half, cc),
            p_s.at[m, half, cc], p_r.at[m, half, cc], r, y * 2 + (1 - xl),
        )

    def keys_home(m, half, cc):
        src, dst = keys_part(sg, m, half, cc), gkvr.at[y * 2 + c]
        zz = blocks[m][half]
        return (
            (zz == b) & (c == cc), src, dst,
            g_s.at[m, half, cc], g_r.at[y * 2 + c], row_of(z, xh, cc), zz,
        )

    def return_aside(m):
        @pl.when(xl != (z + m) % 2)
        def _():
            for half, cc in parts:
                keys_aside(m, half, cc).start()

    def return_home(m):
        @pl.when(xl == (z + m) % 2)
        def _():
            for half, cc in parts:
                keys_aside(m, half, cc).wait_recv()
                at = slice(cc * NR, (cc + 1) * NR)
                total = sg[m, half, at].astype(f32) + pr[m, half, at].astype(f32)
                sg[m, half, at] = total.astype(bf16)
                is_self, *copy = keys_home(m, half, cc)

                @pl.when(jnp.logical_not(is_self))
                def _(copy=copy):
                    remote(*copy).start()

                @pl.when(is_self)
                def _(copy=copy):
                    copy[1][...] = copy[0][...]

    def return_drain(m):
        @pl.when(xl != (z + m) % 2)
        def _():
            for half, cc in parts:
                keys_aside(m, half, cc).wait_send()

        @pl.when(xl == (z + m) % 2)
        def _():
            for half, cc in parts:
                is_self, *copy = keys_home(m, half, cc)

                @pl.when(jnp.logical_not(is_self))
                def _(copy=copy):
                    remote(*copy).wait_send()

    def reduce_step(hf, m, before):
        low, high = slice(0, 64), slice(64, KB)
        if m == 0:
            sr[hf, 0, low] = gb[hf, 0, 0:64].astype(bf16)
            sl[hf, 0, high] = gb[hf, 0, 64:128].astype(bf16)
            pick_r, pick_l = (hf, 0, low), (hf, 0, high)
        else:
            arrived(before)
            if m == 1:
                sr[hf, m, low] = (gb[hf, m, 0:64] + rr[hf, 0, low].astype(f32)).astype(bf16)
                sr[hf, m, high] = gb[hf, m, 64:128].astype(bf16)
                sl[hf, m, low] = gb[hf, m, 128:192].astype(bf16)
                sl[hf, m, high] = (gb[hf, m, 192:256] + rl[hf, 0, high].astype(f32)).astype(bf16)
            else:
                sr[hf, m] = (gb[hf, m, 0:KB] + rr[hf, m - 1].astype(f32)).astype(bf16)
                sl[hf, m] = (gb[hf, m, KB:] + rl[hf, m - 1].astype(f32)).astype(bf16)
            pick_r = pick_l = (hf, m)
        cr = remote(sr.at[pick_r], rr.at[pick_r], rr_s.at[hf, m], rr_r.at[hf, m], right, b)
        cl = remote(sl.at[pick_l], rl.at[pick_l], rl_s.at[hf, m], rl_r.at[hf, m], left, b)
        cr.start()
        cl.start()
        done.extend((cr, cl))
        return cr, cl

    theirs = pl.ds((1 - c) * NR, NR)

    def query_across(hf):
        cp = remote(gqa.at[hf, theirs], gqc.at[hf], qc_s.at[hf], qc_r.at[hf], other, b)
        cp.start()
        done.append(cp)
        return cp

    def query_back(hf, cp):
        cp.wait_recv()

        def add_q(i, carry):
            total = ((gqa[hf, c * NR + i] + gqc[hf, i]) * SCALE).astype(bf16)
            for n in range(2):
                sgq[2 * hf + n, i] = total[:, n * QB : (n + 1) * QB]
            return carry

        lax.fori_loop(0, NR, add_q, 0)
        for n in range(2):
            yy = 2 * hf + n
            send_or_keep(
                y == yy, sgq.at[yy], gqr.at[y], qy_s.at[yy], qy_r.at[y], r, yy * 2 + xl
            )

    def bias_back(hf, pair):
        arrived(pair)
        total = gb[hf, 0, KB:] + rr[hf, 3].astype(f32) + rl[hf, 3].astype(f32)
        total = total.astype(bf16)
        for xx in range(2):
            for n in range(2):
                yy = 2 * hf + n
                sb[xx, yy] = total[xx * 64 : (xx + 1) * 64, n * QB : (n + 1) * QB]
                send_or_keep(
                    (y == yy) & (xh == xx), sb.at[xx, yy], gbr.at[y, xh],
                    b_s.at[xx, yy], b_r.at[y, xh], row_of(z, xx, c), yy * 2 + xl,
                )

    order = ((0, 1), (1, 1), (0, 0), (1, 0), (0, 2), (1, 2), (0, 3), (1, 3))
    sums = {2: ((0, 0),), 3: ((1, 0), (0, 1)), 4: ((1, 1),), 5: ((0, 2),), 6: ((1, 2), (0, 3)), 7: ((1, 3),)}
    reduced = [None, None]
    for n, (hf, m) in enumerate(order):
        score_rows(hf, m, *blocks[m])
        if hf == 1:
            return_aside(m)
        for part in sums.get(n, ()):
            reduced[part[0]] = reduce_step(*part, reduced[part[0]])
        if n == 0:
            second = ring(1, 3, second)
        if n == 1:
            for pair in first:
                arrived(pair)
        if n == 2:
            for pair in second:
                arrived(pair)
        if n == 4:
            return_home(1)
        if n == 6:
            return_home(0)
            q_pass = query_across(0)
    q_pass_1 = query_across(1)
    return_home(2)
    query_back(0, q_pass)
    query_back(1, q_pass_1)
    bias_back(0, reduced[0])
    bias_back(1, reduced[1])
    return_home(3)

    for n in range(8):

        @pl.when(n != y * 2 + c)
        def _(n=n):
            remote(sg.at[0, 0, 0:NR], gkvr.at[n], g_s.at[0, 0, 0], g_r.at[n], r, b).wait_recv()

    for n in range(NY):

        @pl.when(n != y)
        def _(n=n):
            remote(sgq.at[0], gqr.at[n], qy_s.at[0], qy_r.at[n], r, b).wait_recv()

        for xx in range(2):

            @pl.when((n != y) | (xx != xh))
            def _(n=n, xx=xx):
                remote(sb.at[0, 0], gbr.at[n, xx], b_s.at[0, 0], b_r.at[n, xx], r, b).wait_recv()

    for m in range(4):
        return_drain(m)

    for is_self, *copy in later:

        @pl.when(jnp.logical_not(is_self))
        def _(copy=copy):
            remote(*copy).wait_send()

    done.extend((*e_copies, *w_copies, *c_copies))
    for cp in (*done, *y_copies.values(), *x_copies.values()):
        cp.wait_send()


def home(gqr, gkvr, gbr, gq_ref, gk_ref, gv_ref, gb_ref):
    for i in range(NR):
        gq_ref[i] = jnp.concatenate([gqr[h, i].astype(f32) for h in range(H)], 0).T
        for cc in range(2):
            for ref, lo in ((gk_ref, 0), (gv_ref, 32)):
                heads = [gkvr[h * 2 + cc, i, lo : lo + 32].astype(f32) for h in range(H)]
                part = jnp.concatenate(heads, 0).T
                ref[i, cc * 64 : cc * 64 + 64] = part[0:64]
                ref[i, 128 + cc * 64 : 192 + cc * 64] = part[64:128]
    for h in range(H):
        gb_ref[h] = gbr[h, 0].astype(f32) + gbr[h, 1].astype(f32)


def per_device(query, key_in, value, output, dout, lse, bias, mask):
    dma = pltpu.SemaphoreType.DMA
    vmem = pl.BlockSpec(memory_space=pltpu.VMEM)
    scratch = [
        pltpu.VMEM((H, 64, QB), bf16),
        pltpu.VMEM((H, NR, 80, QB), bf16),
        pltpu.VMEM((H, 2, NR, 64, KB), bf16),
        pltpu.VMEM((2, NZ, KB, HJ), bf16),
        pltpu.VMEM((2 * NR, 128, NJ), bf16),
        pltpu.VMEM((NZ, 2 * NR, 64, KB), bf16),
        pltpu.VMEM((NZ, 1, KB), f32),
        pltpu.VMEM((NZ, 2 * NR, 2 * KB, 128), bf16),
        pltpu.VMEM((2, 4, 2 * KB, HJ), f32),
        pltpu.VMEM((2, 4, KB, HJ), bf16),
        pltpu.VMEM((2, 4, KB, HJ), bf16),
        pltpu.VMEM((2, 4, KB, HJ), bf16),
        pltpu.VMEM((2, 4, KB, HJ), bf16),
        pltpu.VMEM((2, 2 * NR, DH, HJ), f32),
        pltpu.VMEM((4, 2 * NR, 64, 2 * KB), f32),
        pltpu.VMEM((4, 2, 2 * NR, 64, KB), bf16),
        pltpu.VMEM((4, 2, 2 * NR, 64, KB), bf16),
        pltpu.VMEM((2, NR, DH, HJ), f32),
        pltpu.VMEM((NY, NR, DH, QB), bf16),
        pltpu.VMEM((2, NY, 64, QB), bf16),
    ]
    four, pair, ring = dma((4,)), dma((2, 4)), dma((2, 4, 2))
    sems = [
        dma((8,)), dma((8,)), four, four, four, four, dma((8,)), dma((8,)), four, four,
        ring, ring, ring, ring,
        pair, pair, pair, pair, dma((4, 2, 2)), dma((4, 2, 2)), dma((4, 2, 2)), dma((8,)), dma((2,)), dma((2,)),
        four, four, pair, dma((4, 2)), four,
    ]
    gqr, gkvr, gbr = pl.pallas_call(
        kernel,
        out_shape=[
            jax.ShapeDtypeStruct((NY, NR, DH, QB), bf16),
            jax.ShapeDtypeStruct((8, NR, 64, KB), bf16),
            jax.ShapeDtypeStruct((NY, 2, 64, QB), bf16),
        ],
        in_specs=[vmem] * 8,
        out_specs=[vmem] * 3,
        scratch_shapes=scratch + sems,
        compiler_params=pltpu.CompilerParams(
            collective_id=0, has_side_effects=True, vmem_limit_bytes=56 << 20
        ),
    )(
        query, key_in, value, output, dout,
        lse.transpose(1, 0, 2), bias.transpose(0, 2, 1), mask.reshape(1, -1),
    )
    grad = jax.ShapeDtypeStruct(query.shape, f32)
    gq, gk, gv, gb = pl.pallas_call(
        home,
        out_shape=[grad, grad, grad, jax.ShapeDtypeStruct((H, 64, QB), f32)],
        in_specs=[vmem] * 3,
        out_specs=[vmem] * 4,
    )(gqr, gkvr, gbr)
    return gq, gk, gv, gb.transpose(0, 2, 1)


def solution(mesh):
    in_specs = (
        P("row", "key", None),
        P("row", "key", None),
        P("row", "key", None),
        P("row", "key", None),
        P("row", "key", None),
        P(None, "row", "key"),
        P(None, "key", "row"),
        P(),
    )
    out_specs = (
        P("row", "key", None),
        P("row", "key", None),
        P("row", "key", None),
        P(None, "key", "row"),
    )
    return jax.shard_map(
        per_device, mesh=mesh, in_specs=in_specs, out_specs=out_specs, check_vma=False
    )
```
